32 devices in a mesh: sample: 8 (over z, y), space: 4 (over x, core).
Axes of the slice: x: 2, y: 2, z: 4, core: 2. Of those that a mesh axis runs over, the one named last changes fastest.
Arguments:
- volumes: bfloat16 [8, 32, 64, 1024], P('sample', None, 'space'), may hold values from -6 to 6
- first_weight: bfloat16 [64, 864], replicated, may hold values from -0.21875 to 0.21875
- first_bias: float32 [64], replicated, may hold values from -3 to 3
- second_weight: bfloat16 [128, 1728], replicated, may hold values from -0.15625 to 0.15625
- second_bias: float32 [128], replicated, may hold values from -3 to 3
- cotangent: bfloat16 [8, 128, 32, 256], P('sample', None, 'space'), may hold values from -6 to 6
Outputs:
- activation: bfloat16 [8, 128, 32, 256], P('sample', None, 'space')
- input_grad: bfloat16 [8, 32, 64, 1024], P('sample', None, 'space')
- first_wgrad: float32 [64, 864], replicated
- first_bgrad: float32 [64], replicated
- second_wgrad: float32 [128, 1728], replicated
- second_bgrad: float32 [128], replicated
The draws below stay inside these ranges and needn't reach their ends.
All inputs are finite; a program needn't handle non-finite values.
Results may differ from the reference program's by a relative error of at most 0.013.
Values may be sent and summed in bfloat16 or wider, within the bound.
A program may use at most 128 MiB of HBM per device.

```python
import math
import jax
import jax.numpy as jnp
from jax import lax

CH_IN = 32
CH_MID = 64
CH_OUT = 128
VOL_DEPTH = 64
VOL_HEIGHT = 64
VOL_WIDTH = 16
SAMPLES = 8
PLANE = 1024


def block_levels(rng, shape, split, low, largest):
    def one(position, parts):
        draws = jax.random.uniform(jax.random.fold_in(jax.random.fold_in(rng, 6), position), (parts,), jnp.float32, low / len(split), largest / len(split))
        return jnp.repeat(jnp.exp(draws), shape[position] // parts).reshape((-1,) + (1,) * (len(shape) - position - 1))

    loudness = one(*split[0])
    for cut in split[1:]:
        loudness = loudness * one(*cut)
    return loudness


def centred(own_key, extent, spread, reach, split=(), dtype=jnp.bfloat16):
    values = jax.random.normal(own_key, extent, jnp.float32) * spread
    if len(split) > 0:
        values = block_levels(own_key, extent, split, -0.22, 0.18) * values
    return jnp.clip(values, min=-reach, max=reach).astype(dtype)


def setup_inputs(seed: int = 0) -> dict:
    splits = jax.random.split(jax.random.key(seed), 7)
    volumes = centred(splits[0], (SAMPLES, CH_IN, VOL_DEPTH, PLANE), 1.0, 6.0, ((0, 8), (2, 4)))
    first_weight = centred(splits[1], (CH_MID, 27 * CH_IN), (27 * CH_IN) ** -0.5, 0.21875)
    first_bias = centred(splits[2], (CH_MID,), 0.5, 3.0, (), jnp.float32)
    second_weight = centred(splits[3], (CH_OUT, 27 * CH_MID), (27 * CH_MID) ** -0.5, 0.15625)
    second_bias = centred(splits[4], (CH_OUT,), 0.5, 3.0, (), jnp.float32)
    cotangent = centred(splits[5], (SAMPLES, CH_OUT, VOL_DEPTH // 2, PLANE // 4), 1.0, 6.0, ((0, 8), (2, 4)))
    return {"volumes": volumes, "first_weight": first_weight, "first_bias": first_bias, "second_weight": second_weight, "second_bias": second_bias, "cotangent": cotangent}


LAYOUT_SPEC = ('NCDHW', 'OIDHW', 'NCDHW')

def kernel_of(weight, channels):
    return weight.astype(jnp.float32).reshape(weight.shape[0], 3, 3, 3, channels).transpose(0, 4, 1, 2, 3)

def flipped(kernel):
    return jnp.flip(kernel, (2, 3, 4)).transpose(1, 0, 2, 3, 4)

def correlate(padded, kernel):
    return lax.conv_general_dilated(padded, kernel, (1, 1, 1), 'VALID', dimension_numbers=LAYOUT_SPEC, precision=lax.Precision.HIGHEST)

def pad_all(volume):
    return jnp.pad(volume, ((0, 0), (0, 0), (1, 1), (1, 1), (1, 1)))

def silu_slope(values_in):
    sigmoid_v = jax.nn.sigmoid(values_in)
    return sigmoid_v * (1.0 + values_in * (1.0 - sigmoid_v))

def upsampled(pooled_grad, slope):
    sample_count, channels, planes, rows_half, cols_half = pooled_grad.shape
    shaped = slope.reshape(sample_count, channels, planes, 2, rows_half, 2, cols_half, 2)
    return (pooled_grad[:, :, :, None, :, None, :, None] * 0.125 * shaped).reshape(slope.shape)

def weight_grad(padded, slope_grad):
    depth_cells, height_cells, width_cells = slope_grad.shape[2:]
    columns = []
    for offset in range(27):
        depth_off, height_off, width_off = (offset // 9, offset // 3 % 3, offset % 3)
        window = padded[:, :, depth_off:depth_off + depth_cells, height_off:height_off + height_cells, width_off:width_off + width_cells]
        columns.append(lax.dot_general(slope_grad, window, (((0, 2, 3, 4), (0, 2, 3, 4)), ((), ())), precision=lax.Precision.HIGHEST))
    return jnp.concatenate(columns, axis=1)

def one_sample(volume, cot_sample, first_weight, first_bias, second_weight, second_bias):
    inputs = volume.astype(jnp.float32).reshape(1, CH_IN, VOL_DEPTH, VOL_HEIGHT, VOL_WIDTH)
    kernel_one = kernel_of(first_weight, CH_IN)
    kernel_two = kernel_of(second_weight, CH_MID)
    padded_in = pad_all(inputs)
    first_pre = correlate(padded_in, kernel_one) + first_bias.reshape(1, CH_MID, 1, 1, 1)
    pooled = jax.nn.silu(first_pre).reshape(1, CH_MID, VOL_DEPTH // 2, 2, VOL_HEIGHT // 2, 2, VOL_WIDTH // 2, 2).mean(axis=(3, 5, 7)).astype(jnp.bfloat16)
    padded_pool = pad_all(pooled.astype(jnp.float32))
    second_pre = correlate(padded_pool, kernel_two) + second_bias.reshape(1, CH_OUT, 1, 1, 1)
    activation = jax.nn.silu(second_pre).astype(jnp.bfloat16)
    cot_cells = cot_sample.astype(jnp.float32).reshape(1, CH_OUT, VOL_DEPTH // 2, VOL_HEIGHT // 2, VOL_WIDTH // 2)
    second_grad = (cot_cells * silu_slope(second_pre)).astype(jnp.bfloat16).astype(jnp.float32)
    pooled_grad = correlate(pad_all(second_grad), flipped(kernel_two))
    first_grad = upsampled(pooled_grad, silu_slope(first_pre)).astype(jnp.bfloat16).astype(jnp.float32)
    input_grad = correlate(pad_all(first_grad), flipped(kernel_one)).astype(jnp.bfloat16)
    return (activation.reshape(CH_OUT, VOL_DEPTH // 2, PLANE // 4), input_grad.reshape(CH_IN, VOL_DEPTH, PLANE), weight_grad(padded_in, first_grad), lax.optimization_barrier(jnp.sum(first_grad, axis=(0, 2, 3, 4))), weight_grad(padded_pool, second_grad), lax.optimization_barrier(jnp.sum(second_grad, axis=(0, 2, 3, 4))))

def reference(volumes, first_weight, first_bias, second_weight, second_bias, cotangent):

    def one_step(sample_pair):
        return one_sample(sample_pair[0], sample_pair[1], first_weight, first_bias, second_weight, second_bias)
    results = lax.map(one_step, (volumes, cotangent))
    factor = 1.0 / math.sqrt(SAMPLES * VOL_DEPTH * VOL_HEIGHT * VOL_WIDTH / 8.0)
    return (results[0], results[1], lax.optimization_barrier(jnp.sum(results[2], axis=0)) * factor, lax.optimization_barrier(jnp.sum(results[3], axis=0)) * factor, lax.optimization_barrier(jnp.sum(results[4], axis=0)) * factor, lax.optimization_barrier(jnp.sum(results[5], axis=0)) * factor)
```

```python
import functools
import math

import jax
import jax.numpy as jnp
import numpy as np
from jax import lax
from jax.experimental import pallas as pl
from jax.experimental.pallas import tpu as pltpu
from jax.sharding import PartitionSpec as P

CH_IN = 32
CH_MID = 64
CH_OUT = 128
VOL_HEIGHT = 64
VOL_WIDTH = 16

VMEM_BYTES = 56 * 1024 * 1024
BF = jnp.bfloat16
F32 = jnp.float32


def tap_masks(height, width):
    rows = np.arange(height * width) // width
    cols = np.arange(height * width) % width
    out = []
    for tap in range(9):
        up, side = tap // 3 - 1, tap % 3 - 1
        good = (rows + up >= 0) & (rows + up < height) & (cols + side >= 0) & (cols + side < width)
        out.append(np.repeat(good[None], 16, 0))
    return jnp.asarray(np.concatenate(out).astype(np.float32), BF)


def pool_matrix():
    cell = np.arange(32 * VOL_WIDTH)
    target = (cell // VOL_WIDTH // 2) * (VOL_WIDTH // 2) + cell % VOL_WIDTH // 2
    return (target[:, None] == np.arange(128)[None]).astype(np.float32) * 0.125


def banded(weight, planes):
    taps = weight.shape[1] // 3
    return jnp.concatenate(
        [jnp.pad(weight, ((0, 0), (j * taps, (planes - 1 - j) * taps))) for j in range(planes)]
    )


def turned(weight, channels):
    outs = weight.shape[0]
    return weight.reshape(outs, 27, channels)[:, ::-1].transpose(2, 1, 0).reshape(channels, 27 * outs)


def put_columns(x, base, col, mask, width):
    channels, cells = x.shape
    for tap in range(9):
        by = (tap // 3 - 1) * width + tap % 3 - 1
        moved = x
        if by:
            good = mask[tap * 16 : (tap + 1) * 16, :]
            moved = pltpu.roll(x, (-by) % cells, 1) * jnp.concatenate([good] * (channels // 16), 0)
        start = pl.multiple_of(base + tap * channels, 16)
        col[pl.ds(start, channels), :] = moved


def fill_columns(before, x, after, col, mask, channels, width):
    planes = x.shape[0] // channels
    put_columns(before[...], 0, col, mask, width)
    put_columns(after[...], (planes + 1) * 9 * channels, col, mask, width)

    def body(p, carry):
        start = pl.multiple_of(p * channels, channels)
        put_columns(x[pl.ds(start, channels), :], (p + 1) * (9 * channels), col, mask, width)
        return carry

    lax.fori_loop(0, planes, body, 0)


def sigmoid(v):
    return 0.5 * jnp.tanh(0.5 * v) + 0.5


def first_kernel(before, x, after, weight, bias, mask, pool, pooled, slope, col):
    fill_columns(before, x, after, col, mask, CH_IN, VOL_WIDTH)
    group = weight.shape[0] // CH_MID
    taps = 9 * CH_IN
    chunks = x.shape[1] // 512

    def body(step, carry):
        i, n = step // chunks, step % chunks
        lanes = pl.ds(pl.multiple_of(n * 512, 512), 512)
        window = col[pl.ds(pl.multiple_of(i * (group * taps), 16), (group + 2) * taps), lanes]
        pre = jnp.dot(weight[...], window, preferred_element_type=F32) + bias[...]
        s = sigmoid(pre)
        act = pre * s
        rows = pl.ds(pl.multiple_of(i * (group * CH_MID), 64), group * CH_MID)
        slope[rows, lanes] = (s + act * (1.0 - s)).astype(BF)
        sums = jnp.concatenate(
            [
                act[2 * j * CH_MID : (2 * j + 1) * CH_MID] + act[(2 * j + 1) * CH_MID : (2 * j + 2) * CH_MID]
                for j in range(group // 2)
            ]
        ).astype(BF)
        half = pl.ds(pl.multiple_of(i * (group // 2 * CH_MID), 64), group // 2 * CH_MID)
        small = pl.ds(pl.multiple_of(n * 128, 128), 128)
        pooled[half, small] = jnp.dot(sums, pool[...], preferred_element_type=F32).astype(BF)
        return carry

    lax.fori_loop(0, x.shape[0] // (group * CH_IN) * chunks, body, 0)


def second_kernel(before, x, after, weight, bias, cot, mask, act_out, grad_out, col):
    fill_columns(before, x, after, col, mask, CH_MID, VOL_WIDTH // 2)
    group = weight.shape[0] // CH_OUT
    taps = 9 * CH_MID

    def body(i, carry):
        window = col[pl.ds(pl.multiple_of(i * (group * taps), 16), (group + 2) * taps), :]
        pre = jnp.dot(weight[...], window, preferred_element_type=F32) + bias[...]
        s = sigmoid(pre)
        act = pre * s
        rows = pl.ds(pl.multiple_of(i * (group * CH_OUT), 128), group * CH_OUT)
        act_out[rows, :] = act.astype(BF)
        grad_out[rows, :] = (cot[rows, :].astype(F32) * (s + act * (1.0 - s))).astype(BF)
        return carry

    lax.fori_loop(0, x.shape[0] // (group * CH_MID), body, 0)


def weight_kernel(outs, grad, col, total, wide):
    cells = grad.shape[1]
    planes = grad.shape[0] // outs
    taps = col.shape[0] // (planes + 2)
    edge = jnp.zeros((2 * outs, cells), BF)
    wide[0 : 2 * outs, :] = edge
    wide[(planes + 2) * outs : (planes + 4) * outs, :] = edge
    wide[2 * outs : (planes + 2) * outs, :] = grad[...]
    total[...] = jnp.zeros_like(total)
    ones = jnp.ones((16, cells), BF)

    def body(p, carry):
        left = jnp.concatenate([col[pl.ds(pl.multiple_of(p * taps, 16), taps), :], ones])
        right = wide[pl.ds(pl.multiple_of(p * outs, 64), 3 * outs), :]
        total[...] += lax.dot_general(
            left, right, (((1,), (1,)), ((), ())), preferred_element_type=F32
        )
        return carry

    lax.fori_loop(0, planes + 2, body, 0)


def spread_kernel(before, x, after, weight, mask, spread, slope, grad_out, col):
    fill_columns(before, x, after, col, mask, CH_OUT, VOL_WIDTH // 2)
    group = weight.shape[0] // CH_MID
    taps = 9 * CH_OUT

    def body(i, carry):
        window = col[pl.ds(pl.multiple_of(i * (group * taps), 16), (group + 2) * taps), :]
        pooled_grad = jnp.dot(weight[...], window, preferred_element_type=F32).astype(BF)
        for n in range(x.shape[1] // 128):
            big = jnp.dot(
                pooled_grad[:, n * 128 : (n + 1) * 128], spread[...], preferred_element_type=F32
            )
            for j in range(2 * group):
                rows = pl.ds(pl.multiple_of(i * (2 * group * CH_MID) + j * CH_MID, 64), CH_MID)
                lanes = slice(n * 512, (n + 1) * 512)
                part = big[j // 2 * CH_MID : (j // 2 + 1) * CH_MID]
                grad_out[rows, lanes] = (part * slope[rows, lanes].astype(F32)).astype(BF)
        return carry

    lax.fori_loop(0, x.shape[0] // (group * CH_OUT), body, 0)


def input_kernel(before, x, after, weight, mask, out, col):
    fill_columns(before, x, after, col, mask, CH_MID, VOL_WIDTH)
    group = weight.shape[0] // CH_IN
    taps = 9 * CH_MID
    chunks = x.shape[1] // 256

    def body(step, carry):
        i, n = step // chunks, step % chunks
        lanes = pl.ds(pl.multiple_of(n * 256, 256), 256)
        window = col[pl.ds(pl.multiple_of(i * (group * taps), 16), (group + 2) * taps), lanes]
        rows = pl.ds(pl.multiple_of(i * (group * CH_IN), 32), group * CH_IN)
        out[rows, lanes] = jnp.dot(weight[...], window, preferred_element_type=F32).astype(BF)
        return carry

    lax.fori_loop(0, x.shape[0] // (group * CH_MID) * chunks, body, 0)


def call(kernel, outs, scratch, flops, *operands):
    whole = pl.BlockSpec(memory_space=pltpu.VMEM)
    moved = sum(o.size * o.dtype.itemsize for o in operands)
    return pl.pallas_call(
        kernel,
        out_shape=[jax.ShapeDtypeStruct(shape, dtype) for shape, dtype in outs],
        in_specs=[whole] * len(operands),
        out_specs=[whole] * len(outs),
        scratch_shapes=[pltpu.VMEM(shape, dtype) for shape, dtype in scratch],
        compiler_params=pltpu.CompilerParams(vmem_limit_bytes=VMEM_BYTES),
        cost_estimate=pl.CostEstimate(flops=flops, bytes_accessed=moved, transcendentals=0),
    )(*operands)


def halo(x, rows):
    size = lax.axis_size("space")
    up = [(i, i + 1) for i in range(size - 1)]
    down = [(j, i) for i, j in up]
    before = lax.ppermute(x[x.shape[0] - rows :], "space", up)
    after = lax.ppermute(x[:rows], "space", down)
    return before, after


def group_of(planes, most):
    group = most
    while planes % group:
        group //= 2
    return group


def one_sample(volume, cot, weights, masks, pools):
    planes, cells = volume.shape[1:]
    half, small = planes // 2, cells // 4
    first_w, first_b, second_w, second_b, spread_w, input_w = weights
    big_mask, small_mask = masks
    x = volume.transpose(1, 0, 2).reshape(planes * CH_IN, cells)
    cot = cot.transpose(1, 0, 2).reshape(half * CH_OUT, small)

    work = 2 * planes * cells * 27 * CH_IN * CH_MID
    before, after = halo(x, CH_IN)
    pooled, slope, col = call(
        first_kernel,
        [
            ((half * CH_MID, small), BF),
            ((planes * CH_MID, cells), BF),
            (((planes + 2) * 9 * CH_IN, cells), BF),
        ],
        [],
        4 * work,
        before, x, after, first_w, first_b, big_mask, pools[0],
    )
    before, after = halo(pooled, CH_MID)
    act, grad, small_col = call(
        second_kernel,
        [
            ((half * CH_OUT, small), BF),
            ((half * CH_OUT, small), BF),
            (((half + 2) * 9 * CH_MID, small), BF),
        ],
        [],
        work,
        before, pooled, after, second_w, second_b, cot, small_mask,
    )
    before, after = halo(grad, CH_OUT)
    (second_total,) = call(
        functools.partial(weight_kernel, CH_OUT),
        [((9 * CH_MID + 16, 3 * CH_OUT), F32)],
        [(((half + 4) * CH_OUT, small), BF)],
        2 * work,
        grad, small_col,
    )
    (first_grad,) = call(
        spread_kernel,
        [((planes * CH_MID, cells), BF)],
        [(((half + 2) * 9 * CH_OUT, small), BF)],
        2 * work,
        before, grad, after, spread_w, small_mask, pools[1], slope,
    )
    before, after = halo(first_grad, CH_MID)
    (first_total,) = call(
        functools.partial(weight_kernel, CH_MID),
        [((9 * CH_IN + 16, 3 * CH_MID), F32)],
        [(((planes + 4) * CH_MID, cells), BF)],
        4 * work,
        first_grad, col,
    )
    (input_grad,) = call(
        input_kernel,
        [((planes * CH_IN, cells), BF)],
        [(((planes + 2) * 9 * CH_MID, cells), BF)],
        6 * work,
        before, first_grad, after, input_w, big_mask,
    )
    act = act.reshape(half, CH_OUT, small).transpose(1, 0, 2)
    input_grad = input_grad.reshape(planes, CH_IN, cells).transpose(1, 0, 2)
    return act, input_grad, first_total, second_total


def unpacked(total, outs):
    taps = total.shape[0] - 16
    wgrad = total[:taps].reshape(taps, 3, outs)[:, ::-1].transpose(2, 1, 0).reshape(outs, 3 * taps)
    return wgrad, total[taps, :outs]


def per_device(volumes, first_weight, first_bias, second_weight, second_bias, cotangent):
    samples, _, planes, cells = volumes.shape
    all_samples = samples * lax.axis_size("sample")
    scale = 1.0 / math.sqrt(all_samples * planes * lax.axis_size("space") * cells / 8.0)
    half = planes // 2
    g1, g2 = group_of(planes, 4), group_of(half, 2)
    g3, g4 = group_of(half, 4), group_of(planes, 4)
    weights = (
        banded(first_weight, g1),
        jnp.tile(first_bias, g1).reshape(-1, 1),
        banded(second_weight, g2),
        jnp.tile(second_bias, g2).reshape(-1, 1),
        banded(turned(second_weight, CH_MID), g3),
        banded(turned(first_weight, CH_IN), g4),
    )
    masks = (tap_masks(VOL_HEIGHT, VOL_WIDTH), tap_masks(VOL_HEIGHT // 2, VOL_WIDTH // 2))
    pool = pool_matrix()
    pools = (jnp.asarray(pool, BF), jnp.asarray(pool.T, BF))
    parts = [one_sample(volumes[s], cotangent[s], weights, masks, pools) for s in range(samples)]
    acts, inputs, firsts, seconds = zip(*parts)
    second_total = lax.psum(sum(seconds[1:], seconds[0]), ("sample", "space"))
    first_total = lax.psum(sum(firsts[1:], firsts[0]), ("sample", "space"))
    first_wgrad, first_bgrad = unpacked(first_total * scale, CH_MID)
    second_wgrad, second_bgrad = unpacked(second_total * scale, CH_OUT)
    return (
        jnp.stack(acts),
        jnp.stack(inputs),
        first_wgrad,
        first_bgrad,
        second_wgrad,
        second_bgrad,
    )


def solution(mesh):
    split = P("sample", None, "space", None)
    return jax.shard_map(
        per_device,
        mesh=mesh,
        in_specs=(split, P(), P(), P(), P(), split),
        out_specs=(split, split, P(), P(), P(), P()),
        check_vma=False,
    )
```

```python
import functools
import math

import jax
import jax.numpy as jnp
import numpy as np
from jax import lax
from jax.experimental import pallas as pl
from jax.experimental.pallas import tpu as pltpu
from jax.sharding import PartitionSpec as P

CH_IN = 32
CH_MID = 64
CH_OUT = 128
VOL_HEIGHT = 64
VOL_WIDTH = 16

VMEM_BYTES = 56 * 1024 * 1024
BF = jnp.bfloat16
F32 = jnp.float32


def tap_masks(height, width):
    rows = np.arange(height * width) // width
    cols = np.arange(height * width) % width
    out = []
    for tap in range(9):
        up, side = tap // 3 - 1, tap % 3 - 1
        good = (rows + up >= 0) & (rows + up < height) & (cols + side >= 0) & (cols + side < width)
        out.append(np.repeat(good[None], 16, 0))
    return jnp.asarray(np.concatenate(out).astype(np.float32), BF)


def pool_matrix():
    cell = np.arange(32 * VOL_WIDTH)
    target = (cell // VOL_WIDTH // 2) * (VOL_WIDTH // 2) + cell % VOL_WIDTH // 2
    return (target[:, None] == np.arange(128)[None]).astype(np.float32) * 0.125


def banded(weight, planes):
    taps = weight.shape[1] // 3
    return jnp.concatenate(
        [jnp.pad(weight, ((0, 0), (j * taps, (planes - 1 - j) * taps))) for j in range(planes)]
    )


def turned(weight, channels):
    outs = weight.shape[0]
    return weight.reshape(outs, 27, channels)[:, ::-1].transpose(2, 1, 0).reshape(channels, 27 * outs)


def put_columns(x, base, col, mask, width):
    channels, cells = x.shape
    for tap in range(9):
        by = (tap // 3 - 1) * width + tap % 3 - 1
        moved = x
        if by:
            good = mask[tap * 16 : (tap + 1) * 16, :]
            moved = pltpu.roll(x, (-by) % cells, 1) * jnp.concatenate([good] * (channels // 16), 0)
        start = pl.multiple_of(base + tap * channels, 16)
        col[pl.ds(start, channels), :] = moved


def fill_columns(before, x, after, col, mask, channels, width):
    planes = x.shape[0] // channels
    put_columns(before[...], 0, col, mask, width)
    put_columns(after[...], (planes + 1) * 9 * channels, col, mask, width)

    def body(p, carry):
        start = pl.multiple_of(p * channels, channels)
        put_columns(x[pl.ds(start, channels), :], (p + 1) * (9 * channels), col, mask, width)
        return carry

    lax.fori_loop(0, planes, body, 0)


def sigmoid(v):
    return 0.5 * jnp.tanh(0.5 * v) + 0.5


def first_kernel(before, x, after, weight, bias, mask, pool, pooled, slope, col):
    fill_columns(before, x, after, col, mask, CH_IN, VOL_WIDTH)
    group = weight.shape[0] // CH_MID
    taps = 9 * CH_IN
    chunks = x.shape[1] // 512

    def body(step, carry):
        i, n = step // chunks, step % chunks
        lanes = pl.ds(pl.multiple_of(n * 512, 512), 512)
        window = col[pl.ds(pl.multiple_of(i * (group * taps), 16), (group + 2) * taps), lanes]
        pre = jnp.dot(weight[...], window, preferred_element_type=F32) + bias[...]
        s = sigmoid(pre)
        act = pre * s
        rows = pl.ds(pl.multiple_of(i * (group * CH_MID), 64), group * CH_MID)
        slope[rows, lanes] = (s + act * (1.0 - s)).astype(BF)
        sums = jnp.concatenate(
            [
                act[2 * j * CH_MID : (2 * j + 1) * CH_MID] + act[(2 * j + 1) * CH_MID : (2 * j + 2) * CH_MID]
                for j in range(group // 2)
            ]
        ).astype(BF)
        half = pl.ds(pl.multiple_of(i * (group // 2 * CH_MID), 64), group // 2 * CH_MID)
        small = pl.ds(pl.multiple_of(n * 128, 128), 128)
        pooled[half, small] = jnp.dot(sums, pool[...], preferred_element_type=F32).astype(BF)
        return carry

    lax.fori_loop(0, x.shape[0] // (group * CH_IN) * chunks, body, 0)


def second_kernel(before, x, after, weight, bias, cot, mask, act_out, grad_out, col):
    fill_columns(before, x, after, col, mask, CH_MID, VOL_WIDTH // 2)
    group = weight.shape[0] // CH_OUT
    taps = 9 * CH_MID

    def body(i, carry):
        window = col[pl.ds(pl.multiple_of(i * (group * taps), 16), (group + 2) * taps), :]
        pre = jnp.dot(weight[...], window, preferred_element_type=F32) + bias[...]
        s = sigmoid(pre)
        act = pre * s
        rows = pl.ds(pl.multiple_of(i * (group * CH_OUT), 128), group * CH_OUT)
        act_out[rows, :] = act.astype(BF)
        grad_out[rows, :] = (cot[rows, :].astype(F32) * (s + act * (1.0 - s))).astype(BF)
        return carry

    lax.fori_loop(0, x.shape[0] // (group * CH_MID), body, 0)


def weight_kernel(outs, grad, col, total, wide):
    cells = grad.shape[1]
    planes = grad.shape[0] // outs
    taps = col.shape[0] // (planes + 2)
    edge = jnp.zeros((2 * outs, cells), BF)
    wide[0 : 2 * outs, :] = edge
    wide[(planes + 2) * outs : (planes + 4) * outs, :] = edge
    wide[2 * outs : (planes + 2) * outs, :] = grad[...]
    total[...] = jnp.zeros_like(total)
    ones = jnp.ones((16, cells), BF)

    def body(p, carry):
        left = jnp.concatenate([col[pl.ds(pl.multiple_of(p * taps, 16), taps), :], ones])
        right = wide[pl.ds(pl.multiple_of(p * outs, 64), 3 * outs), :]
        total[...] += lax.dot_general(
            left, right, (((1,), (1,)), ((), ())), preferred_element_type=F32
        )
        return carry

    lax.fori_loop(0, planes + 2, body, 0)


def spread_kernel(before, x, after, weight, mask, spread, slope, grad_out, col):
    fill_columns(before, x, after, col, mask, CH_OUT, VOL_WIDTH // 2)
    group = weight.shape[0] // CH_MID
    taps = 9 * CH_OUT

    def body(i, carry):
        window = col[pl.ds(pl.multiple_of(i * (group * taps), 16), (group + 2) * taps), :]
        pooled_grad = jnp.dot(weight[...], window, preferred_element_type=F32).astype(BF)
        for n in range(x.shape[1] // 128):
            big = jnp.dot(
                pooled_grad[:, n * 128 : (n + 1) * 128], spread[...], preferred_element_type=F32
            )
            for j in range(2 * group):
                rows = pl.ds(pl.multiple_of(i * (2 * group * CH_MID) + j * CH_MID, 64), CH_MID)
                lanes = slice(n * 512, (n + 1) * 512)
                part = big[j // 2 * CH_MID : (j // 2 + 1) * CH_MID]
                grad_out[rows, lanes] = (part * slope[rows, lanes].astype(F32)).astype(BF)
        return carry

    lax.fori_loop(0, x.shape[0] // (group * CH_OUT), body, 0)


def input_kernel(before, x, after, weight, mask, out, col):
    fill_columns(before, x, after, col, mask, CH_MID, VOL_WIDTH)
    group = weight.shape[0] // CH_IN
    taps = 9 * CH_MID
    chunks = x.shape[1] // 256

    def body(step, carry):
        i, n = step // chunks, step % chunks
        lanes = pl.ds(pl.multiple_of(n * 256, 256), 256)
        window = col[pl.ds(pl.multiple_of(i * (group * taps), 16), (group + 2) * taps), lanes]
        rows = pl.ds(pl.multiple_of(i * (group * CH_IN), 32), group * CH_IN)
        out[rows, lanes] = jnp.dot(weight[...], window, preferred_element_type=F32).astype(BF)
        return carry

    lax.fori_loop(0, x.shape[0] // (group * CH_MID) * chunks, body, 0)


def call(kernel, outs, scratch, flops, *operands):
    whole = pl.BlockSpec(memory_space=pltpu.VMEM)
    moved = sum(o.size * o.dtype.itemsize for o in operands)
    return pl.pallas_call(
        kernel,
        out_shape=[jax.ShapeDtypeStruct(shape, dtype) for shape, dtype in outs],
        in_specs=[whole] * len(operands),
        out_specs=[whole] * len(outs),
        scratch_shapes=[pltpu.VMEM(shape, dtype) for shape, dtype in scratch],
        compiler_params=pltpu.CompilerParams(vmem_limit_bytes=VMEM_BYTES),
        cost_estimate=pl.CostEstimate(flops=flops, bytes_accessed=moved, transcendentals=0),
    )(*operands)


def halo(x, rows):
    size = lax.axis_size("space")
    up = [(i, i + 1) for i in range(size - 1)]
    down = [(j, i) for i, j in up]
    before = lax.ppermute(x[x.shape[0] - rows :], "space", up)
    after = lax.ppermute(x[:rows], "space", down)
    return before, after


def group_of(planes, most):
    group = most
    while planes % group:
        group //= 2
    return group


def all_devices():
    return lax.axis_size("sample") * lax.axis_size("space")


def swapped(x, step):
    pairs = [(i, i ^ step) for i in range(all_devices())]
    return lax.ppermute(x.astype(BF), ("sample", "space"), pairs).astype(F32)


def rounded(x):
    return lax.reduce_precision(x, 8, 7)


def doubled(total, step):
    if step >= all_devices():
        return total
    mine = rounded(total)
    return mine + swapped(mine, step)


def is_upper():
    return lax.axis_index("space") % 2 == 1


def halved(total):
    rows = total.shape[0] // 2
    low, high = rounded(total[:rows]), rounded(total[rows:])
    upper = is_upper()
    return jnp.where(upper, high, low) + swapped(jnp.where(upper, low, high), 1)


def joined(part):
    mine = rounded(part)
    other = swapped(mine, 1)
    upper = is_upper()
    return jnp.concatenate([jnp.where(upper, other, mine), jnp.where(upper, mine, other)])


def finished(part, step, last):
    while step < all_devices():
        part = doubled(part, step)
        step *= 2
    return last(part)


def one_sample(volume, cot, weights, masks, pools, alone):
    planes, cells = volume.shape[1:]
    half, small = planes // 2, cells // 4
    first_w, first_b, second_w, second_b, spread_w, input_w = weights
    big_mask, small_mask = masks
    x = volume.transpose(1, 0, 2).reshape(planes * CH_IN, cells)
    cot = cot.transpose(1, 0, 2).reshape(half * CH_OUT, small)

    work = 2 * planes * cells * 27 * CH_IN * CH_MID
    before, after = halo(x, CH_IN)
    pooled, slope, col = call(
        first_kernel,
        [
            ((half * CH_MID, small), BF),
            ((planes * CH_MID, cells), BF),
            (((planes + 2) * 9 * CH_IN, cells), BF),
        ],
        [],
        4 * work,
        before, x, after, first_w, first_b, big_mask, pools[0],
    )
    before, after = halo(pooled, CH_MID)
    act, grad, small_col = call(
        second_kernel,
        [
            ((half * CH_OUT, small), BF),
            ((half * CH_OUT, small), BF),
            (((half + 2) * 9 * CH_MID, small), BF),
        ],
        [],
        work,
        before, pooled, after, second_w, second_b, cot, small_mask,
    )
    before, after = halo(grad, CH_OUT)
    (second_total,) = call(
        functools.partial(weight_kernel, CH_OUT),
        [((9 * CH_MID + 16, 3 * CH_OUT), F32)],
        [(((half + 4) * CH_OUT, small), BF)],
        2 * work,
        grad, small_col,
    )
    if alone:
        second_total = halved(second_total)
    (first_grad,) = call(
        spread_kernel,
        [((planes * CH_MID, cells), BF)],
        [(((half + 2) * 9 * CH_OUT, small), BF)],
        2 * work,
        before, grad, after, spread_w, small_mask, pools[1], slope,
    )
    before, after = halo(first_grad, CH_MID)
    local = first_grad
    if alone:
        local, second_total = lax.optimization_barrier((local, second_total))
        second_total = doubled(second_total, 2)
    (first_total,) = call(
        functools.partial(weight_kernel, CH_MID),
        [((9 * CH_IN + 16, 3 * CH_MID), F32)],
        [(((planes + 4) * CH_MID, cells), BF)],
        4 * work,
        local, col,
    )
    if alone:
        before, second_total = lax.optimization_barrier((before, second_total))
        second_total = doubled(second_total, 4)
        first_total = doubled(first_total, 1)
    (input_grad,) = call(
        input_kernel,
        [((planes * CH_IN, cells), BF)],
        [(((planes + 2) * 9 * CH_MID, cells), BF)],
        6 * work,
        before, first_grad, after, input_w, big_mask,
    )
    act = act.reshape(half, CH_OUT, small).transpose(1, 0, 2)
    input_grad = input_grad.reshape(planes, CH_IN, cells).transpose(1, 0, 2)
    return act, input_grad, first_total, second_total


def unpacked(total, outs):
    taps = total.shape[0] - 16
    wgrad = total[:taps].reshape(taps, 3, outs)[:, ::-1].transpose(2, 1, 0).reshape(outs, 3 * taps)
    return wgrad, total[taps, :outs]


def per_device(volumes, first_weight, first_bias, second_weight, second_bias, cotangent):
    samples, _, planes, cells = volumes.shape
    all_samples = samples * lax.axis_size("sample")
    scale = 1.0 / math.sqrt(all_samples * planes * lax.axis_size("space") * cells / 8.0)
    half = planes // 2
    g1, g2 = group_of(planes, 4), group_of(half, 2)
    g3, g4 = group_of(half, 4), group_of(planes, 4)
    weights = (
        banded(first_weight, g1),
        jnp.tile(first_bias, g1).reshape(-1, 1),
        banded(second_weight, g2),
        jnp.tile(second_bias, g2).reshape(-1, 1),
        banded(turned(second_weight, CH_MID), g3),
        banded(turned(first_weight, CH_IN), g4),
    )
    masks = (tap_masks(VOL_HEIGHT, VOL_WIDTH), tap_masks(VOL_HEIGHT // 2, VOL_WIDTH // 2))
    pool = pool_matrix()
    pools = (jnp.asarray(pool, BF), jnp.asarray(pool.T, BF))
    count = all_devices()
    alone = samples == 1 and count & (count - 1) == 0 and lax.axis_size("space") % 2 == 0
    parts = [
        one_sample(volumes[s], cotangent[s], weights, masks, pools, alone) for s in range(samples)
    ]
    acts, inputs, firsts, seconds = zip(*parts)
    if alone:
        second_total = finished(seconds[0], 8, joined)
        first_total = finished(firsts[0], 2, lambda part: part)
    else:
        second_total = lax.psum(sum(seconds[1:], seconds[0]), ("sample", "space"))
        first_total = lax.psum(sum(firsts[1:], firsts[0]), ("sample", "space"))
    first_wgrad, first_bgrad = unpacked(first_total * scale, CH_MID)
    second_wgrad, second_bgrad = unpacked(second_total * scale, CH_OUT)
    return (
        jnp.stack(acts),
        jnp.stack(inputs),
        first_wgrad,
        first_bgrad,
        second_wgrad,
        second_bgrad,
    )


def solution(mesh):
    split = P("sample", None, "space", None)
    return jax.shard_map(
        per_device,
        mesh=mesh,
        in_specs=(split, P(), P(), P(), P(), split),
        out_specs=(split, split, P(), P(), P(), P()),
        check_vma=False,
    )
```

```python
import functools
import math

import jax
import jax.numpy as jnp
import numpy as np
from jax import lax
from jax.experimental import pallas as pl
from jax.experimental.pallas import tpu as pltpu
from jax.sharding import PartitionSpec as P

CH_IN = 32
CH_MID = 64
CH_OUT = 128
VOL_HEIGHT = 64
VOL_WIDTH = 16

VMEM_BYTES = 56 * 1024 * 1024
BF = jnp.bfloat16
F32 = jnp.float32


def tap_masks(height, width):
    rows = np.arange(height * width) // width
    cols = np.arange(height * width) % width
    out = []
    for tap in range(9):
        up, side = tap // 3 - 1, tap % 3 - 1
        good = (rows + up >= 0) & (rows + up < height) & (cols + side >= 0) & (cols + side < width)
        out.append(np.repeat(good[None], 16, 0))
    return jnp.asarray(np.concatenate(out).astype(np.float32), BF)


def pool_matrix():
    cell = np.arange(32 * VOL_WIDTH)
    target = (cell // VOL_WIDTH // 2) * (VOL_WIDTH // 2) + cell % VOL_WIDTH // 2
    return (target[:, None] == np.arange(128)[None]).astype(np.float32) * 0.125


def banded(weight, planes):
    taps = weight.shape[1] // 3
    return jnp.concatenate(
        [jnp.pad(weight, ((0, 0), (j * taps, (planes - 1 - j) * taps))) for j in range(planes)]
    )


def turned(weight, channels):
    outs = weight.shape[0]
    return weight.reshape(outs, 27, channels)[:, ::-1].transpose(2, 1, 0).reshape(channels, 27 * outs)


def put_columns(x, base, col, mask, width):
    channels, cells = x.shape
    for tap in range(9):
        by = (tap // 3 - 1) * width + tap % 3 - 1
        moved = x
        if by:
            good = mask[tap * 16 : (tap + 1) * 16, :]
            moved = pltpu.roll(x, (-by) % cells, 1) * jnp.concatenate([good] * (channels // 16), 0)
        start = pl.multiple_of(base + tap * channels, 16)
        col[pl.ds(start, channels), :] = moved


def fill_columns(before, x, after, col, mask, channels, width):
    planes = x.shape[0] // channels
    put_columns(before[...], 0, col, mask, width)
    put_columns(after[...], (planes + 1) * 9 * channels, col, mask, width)

    def body(p, carry):
        start = pl.multiple_of(p * channels, channels)
        put_columns(x[pl.ds(start, channels), :], (p + 1) * (9 * channels), col, mask, width)
        return carry

    lax.fori_loop(0, planes, body, 0)


def sigmoid(v):
    return 0.5 * jnp.tanh(0.5 * v) + 0.5


def first_kernel(before, x, after, weight, bias, mask, pool, pooled, slope, col):
    fill_columns(before, x, after, col, mask, CH_IN, VOL_WIDTH)
    group = weight.shape[0] // CH_MID
    taps = 9 * CH_IN
    chunks = x.shape[1] // 512

    def body(step, carry):
        i, n = step // chunks, step % chunks
        lanes = pl.ds(pl.multiple_of(n * 512, 512), 512)
        window = col[pl.ds(pl.multiple_of(i * (group * taps), 16), (group + 2) * taps), lanes]
        pre = jnp.dot(weight[...], window, preferred_element_type=F32) + bias[...]
        s = sigmoid(pre)
        act = pre * s
        rows = pl.ds(pl.multiple_of(i * (group * CH_MID), 64), group * CH_MID)
        slope[rows, lanes] = (s + act * (1.0 - s)).astype(BF)
        sums = jnp.concatenate(
            [
                act[2 * j * CH_MID : (2 * j + 1) * CH_MID] + act[(2 * j + 1) * CH_MID : (2 * j + 2) * CH_MID]
                for j in range(group // 2)
            ]
        ).astype(BF)
        half = pl.ds(pl.multiple_of(i * (group // 2 * CH_MID), 64), group // 2 * CH_MID)
        small = pl.ds(pl.multiple_of(n * 128, 128), 128)
        pooled[half, small] = jnp.dot(sums, pool[...], preferred_element_type=F32).astype(BF)
        return carry

    lax.fori_loop(0, x.shape[0] // (group * CH_IN) * chunks, body, 0)


def second_kernel(before, x, after, weight, bias, cot, mask, act_out, grad_out, col):
    fill_columns(before, x, after, col, mask, CH_MID, VOL_WIDTH // 2)
    group = weight.shape[0] // CH_OUT
    taps = 9 * CH_MID

    def body(i, carry):
        window = col[pl.ds(pl.multiple_of(i * (group * taps), 16), (group + 2) * taps), :]
        pre = jnp.dot(weight[...], window, preferred_element_type=F32) + bias[...]
        s = sigmoid(pre)
        act = pre * s
        rows = pl.ds(pl.multiple_of(i * (group * CH_OUT), 128), group * CH_OUT)
        act_out[rows, :] = act.astype(BF)
        grad_out[rows, :] = (cot[rows, :].astype(F32) * (s + act * (1.0 - s))).astype(BF)
        return carry

    lax.fori_loop(0, x.shape[0] // (group * CH_MID), body, 0)


def weight_kernel(outs, grad, col, total, wide):
    cells = grad.shape[1]
    planes = grad.shape[0] // outs
    taps = col.shape[0] // (planes + 2)
    edge = jnp.zeros((2 * outs, cells), BF)
    wide[0 : 2 * outs, :] = edge
    wide[(planes + 2) * outs : (planes + 4) * outs, :] = edge
    wide[2 * outs : (planes + 2) * outs, :] = grad[...]
    total[...] = jnp.zeros_like(total)
    ones = jnp.ones((16, cells), BF)

    def body(p, carry):
        left = jnp.concatenate([col[pl.ds(pl.multiple_of(p * taps, 16), taps), :], ones])
        right = wide[pl.ds(pl.multiple_of(p * outs, 64), 3 * outs), :]
        total[...] += lax.dot_general(
            left, right, (((1,), (1,)), ((), ())), preferred_element_type=F32
        )
        return carry

    lax.fori_loop(0, planes + 2, body, 0)


def spread_kernel(before, x, after, weight, mask, spread, slope, grad_out, col):
    fill_columns(before, x, after, col, mask, CH_OUT, VOL_WIDTH // 2)
    group = weight.shape[0] // CH_MID
    taps = 9 * CH_OUT

    def body(i, carry):
        window = col[pl.ds(pl.multiple_of(i * (group * taps), 16), (group + 2) * taps), :]
        pooled_grad = jnp.dot(weight[...], window, preferred_element_type=F32).astype(BF)
        for n in range(x.shape[1] // 128):
            big = jnp.dot(
                pooled_grad[:, n * 128 : (n + 1) * 128], spread[...], preferred_element_type=F32
            )
            for j in range(2 * group):
                rows = pl.ds(pl.multiple_of(i * (2 * group * CH_MID) + j * CH_MID, 64), CH_MID)
                lanes = slice(n * 512, (n + 1) * 512)
                part = big[j // 2 * CH_MID : (j // 2 + 1) * CH_MID]
                grad_out[rows, lanes] = (part * slope[rows, lanes].astype(F32)).astype(BF)
        return carry

    lax.fori_loop(0, x.shape[0] // (group * CH_OUT), body, 0)


def input_kernel(before, x, after, weight, mask, out, col):
    fill_columns(before, x, after, col, mask, CH_MID, VOL_WIDTH)
    group = weight.shape[0] // CH_IN
    taps = 9 * CH_MID
    chunks = x.shape[1] // 256

    def body(step, carry):
        i, n = step // chunks, step % chunks
        lanes = pl.ds(pl.multiple_of(n * 256, 256), 256)
        window = col[pl.ds(pl.multiple_of(i * (group * taps), 16), (group + 2) * taps), lanes]
        rows = pl.ds(pl.multiple_of(i * (group * CH_IN), 32), group * CH_IN)
        out[rows, lanes] = jnp.dot(weight[...], window, preferred_element_type=F32).astype(BF)
        return carry

    lax.fori_loop(0, x.shape[0] // (group * CH_MID) * chunks, body, 0)


def call(kernel, outs, scratch, flops, *operands):
    whole = pl.BlockSpec(memory_space=pltpu.VMEM)
    moved = sum(o.size * o.dtype.itemsize for o in operands)
    return pl.pallas_call(
        kernel,
        out_shape=[jax.ShapeDtypeStruct(shape, dtype) for shape, dtype in outs],
        in_specs=[whole] * len(operands),
        out_specs=[whole] * len(outs),
        scratch_shapes=[pltpu.VMEM(shape, dtype) for shape, dtype in scratch],
        compiler_params=pltpu.CompilerParams(vmem_limit_bytes=VMEM_BYTES),
        cost_estimate=pl.CostEstimate(flops=flops, bytes_accessed=moved, transcendentals=0),
    )(*operands)


def halo(x, rows):
    size = lax.axis_size("space")
    up = [(i, i + 1) for i in range(size - 1)]
    down = [(j, i) for i, j in up]
    before = lax.ppermute(x[x.shape[0] - rows :], "space", up)
    after = lax.ppermute(x[:rows], "space", down)
    return before, after


def group_of(planes, most):
    group = most
    while planes % group:
        group //= 2
    return group


def all_devices():
    return lax.axis_size("sample") * lax.axis_size("space")


def swapped(x, step):
    pairs = [(i, i ^ step) for i in range(all_devices())]
    return lax.ppermute(x.astype(BF), ("sample", "space"), pairs).astype(F32)


def rounded(x):
    return lax.reduce_precision(x, 8, 7)


def doubled(total, step):
    if step >= all_devices():
        return total
    mine = rounded(total)
    return mine + swapped(mine, step)


def is_upper():
    return lax.axis_index("space") % 2 == 1


def halved(total):
    rows = total.shape[0] // 2
    low, high = rounded(total[:rows]), rounded(total[rows:])
    upper = is_upper()
    return jnp.where(upper, high, low) + swapped(jnp.where(upper, low, high), 1)


def joined(part):
    mine = rounded(part)
    other = swapped(mine, 1)
    upper = is_upper()
    return jnp.concatenate([jnp.where(upper, other, mine), jnp.where(upper, mine, other)])


def finished(part, step, end, last):
    while step < end:
        part = doubled(part, step)
        step *= 2
    return last(part)


def one_sample(volume, cot, weights, masks, pools, alone):
    planes, cells = volume.shape[1:]
    half, small = planes // 2, cells // 4
    first_w, first_b, second_w, second_b, spread_w, input_w = weights
    big_mask, small_mask = masks
    x = volume.transpose(1, 0, 2).reshape(planes * CH_IN, cells)
    cot = cot.transpose(1, 0, 2).reshape(half * CH_OUT, small)

    work = 2 * planes * cells * 27 * CH_IN * CH_MID
    before, after = halo(x, CH_IN)
    pooled, slope, col = call(
        first_kernel,
        [
            ((half * CH_MID, small), BF),
            ((planes * CH_MID, cells), BF),
            (((planes + 2) * 9 * CH_IN, cells), BF),
        ],
        [],
        4 * work,
        before, x, after, first_w, first_b, big_mask, pools[0],
    )
    before, after = halo(pooled, CH_MID)
    act, grad, small_col = call(
        second_kernel,
        [
            ((half * CH_OUT, small), BF),
            ((half * CH_OUT, small), BF),
            (((half + 2) * 9 * CH_MID, small), BF),
        ],
        [],
        work,
        before, pooled, after, second_w, second_b, cot, small_mask,
    )
    before, after = halo(grad, CH_OUT)
    (second_total,) = call(
        functools.partial(weight_kernel, CH_OUT),
        [((9 * CH_MID + 16, 3 * CH_OUT), F32)],
        [(((half + 4) * CH_OUT, small), BF)],
        2 * work,
        grad, small_col,
    )
    if alone:
        second_total = halved(second_total)
    (first_grad,) = call(
        spread_kernel,
        [((planes * CH_MID, cells), BF)],
        [(((half + 2) * 9 * CH_OUT, small), BF)],
        2 * work,
        before, grad, after, spread_w, small_mask, pools[1], slope,
    )
    before, after = halo(first_grad, CH_MID)
    local = first_grad
    if alone:
        local, second_total = lax.optimization_barrier((local, second_total))
        second_total = doubled(second_total, all_devices() // 4)
    (first_total,) = call(
        functools.partial(weight_kernel, CH_MID),
        [((9 * CH_IN + 16, 3 * CH_MID), F32)],
        [(((planes + 4) * CH_MID, cells), BF)],
        4 * work,
        local, col,
    )
    if alone:
        before, first_total, second_total = lax.optimization_barrier(
            (before, first_total, second_total)
        )
        second_total = doubled(second_total, all_devices() // 2)
        first_total = doubled(first_total, all_devices() // 2)
    (input_grad,) = call(
        input_kernel,
        [((planes * CH_IN, cells), BF)],
        [(((planes + 2) * 9 * CH_MID, cells), BF)],
        6 * work,
        before, first_grad, after, input_w, big_mask,
    )
    if alone:
        input_grad, first_total, second_total = lax.optimization_barrier(
            (input_grad, first_total, second_total)
        )
    act = act.reshape(half, CH_OUT, small).transpose(1, 0, 2)
    input_grad = input_grad.reshape(planes, CH_IN, cells).transpose(1, 0, 2)
    return act, input_grad, first_total, second_total


def unpacked(total, outs):
    taps = total.shape[0] - 16
    wgrad = total[:taps].reshape(taps, 3, outs)[:, ::-1].transpose(2, 1, 0).reshape(outs, 3 * taps)
    return wgrad, total[taps, :outs]


def per_device(volumes, first_weight, first_bias, second_weight, second_bias, cotangent):
    samples, _, planes, cells = volumes.shape
    all_samples = samples * lax.axis_size("sample")
    scale = 1.0 / math.sqrt(all_samples * planes * lax.axis_size("space") * cells / 8.0)
    half = planes // 2
    g1, g2 = group_of(planes, 4), group_of(half, 2)
    g3, g4 = group_of(half, 4), group_of(planes, 4)
    weights = (
        banded(first_weight, g1),
        jnp.tile(first_bias, g1).reshape(-1, 1),
        banded(second_weight, g2),
        jnp.tile(second_bias, g2).reshape(-1, 1),
        banded(turned(second_weight, CH_MID), g3),
        banded(turned(first_weight, CH_IN), g4),
    )
    masks = (tap_masks(VOL_HEIGHT, VOL_WIDTH), tap_masks(VOL_HEIGHT // 2, VOL_WIDTH // 2))
    pool = pool_matrix()
    pools = (jnp.asarray(pool, BF), jnp.asarray(pool.T, BF))
    count = all_devices()
    alone = samples == 1 and count >= 8 and count & (count - 1) == 0 and lax.axis_size("space") % 2 == 0
    parts = [
        one_sample(volumes[s], cotangent[s], weights, masks, pools, alone) for s in range(samples)
    ]
    acts, inputs, firsts, seconds = zip(*parts)
    if alone:
        second_total = finished(seconds[0], 2, count // 4, joined)
        first_total = finished(firsts[0], 1, count // 2, lambda part: part)
    else:
        second_total = lax.psum(sum(seconds[1:], seconds[0]), ("sample", "space"))
        first_total = lax.psum(sum(firsts[1:], firsts[0]), ("sample", "space"))
    first_wgrad, first_bgrad = unpacked(first_total * scale, CH_MID)
    second_wgrad, second_bgrad = unpacked(second_total * scale, CH_OUT)
    return (
        jnp.stack(acts),
        jnp.stack(inputs),
        first_wgrad,
        first_bgrad,
        second_wgrad,
        second_bgrad,
    )


def solution(mesh):
    split = P("sample", None, "space", None)
    return jax.shard_map(
        per_device,
        mesh=mesh,
        in_specs=(split, P(), P(), P(), P(), split),
        out_specs=(split, split, P(), P(), P(), P()),
        check_vma=False,
    )
```
